32 devices in a mesh: dp: 16 (over z, y, core), space: 2 (over x).
Axes of the slice: x: 2, y: 2, z: 4, core: 2. Of those that a mesh axis runs over, the one named last changes fastest.
Arguments:
- volume: float32 [16, 32, 8, 256], P('dp', None, 'space'), may hold values from -6 to 6
- cotangent: float32 [16, 64, 32], P('dp', 'space'), may hold values from -6 to 6
- w_first: float32 [64, 2048], replicated, may hold values from -0.125 to 0.125
- b_first: float32 [64], replicated, may hold values from -3 to 3
- w_second: float32 [64, 4096], P('space'), may hold values from -0.09375 to 0.09375
- b_second: float32 [64], P('space'), may hold values from -3 to 3
Outputs:
- output: float32 [16, 64, 32], P('dp', 'space')
- grad_volume: float32 [16, 32, 8, 256], P('dp', None, 'space')
- grad_w_first: float32 [64, 2048], replicated
- grad_b_first: float32 [64], replicated
- grad_w_second: float32 [64, 4096], P('space')
- grad_b_second: float32 [64], P('space')
The draws below stay inside these ranges and needn't reach their ends.
All inputs are finite; a program needn't handle non-finite values.
Results may differ from the reference program's by a relative error of at most 0.00018.
Values sent between devices are 32-bit elements; how exact they have to be, the bound alone decides.
No kernel may reach another device: no remote copies, remote signals or barrier semaphores. Data moves between devices by JAX's collectives and lax.ppermute only.
A program may use at most 128 MiB of HBM per device.

```python
import jax
import jax.numpy as jnp
from jax import lax

CIN = 32
C1 = 64
C2 = 64
HEIGHT = 16
WIDTH = 16
SAMPLES = 16
DEPTH = 8


def shard_levels(stream_key, extent, shards, low, top_value):
    gain, own = 1.0, jax.random.fold_in(stream_key, 6)
    for dim, blocks in shards:
        heights = jnp.exp(jax.random.uniform(jax.random.fold_in(own, dim), (blocks,), jnp.float32, low / len(shards), top_value / len(shards)))
        gain = gain * jnp.repeat(heights, extent[dim] // blocks).reshape([-1 if axis == dim else 1 for axis in range(len(extent))])
    return gain


def bell_draw(stream_key, extent, spread, most, split=(), kind=jnp.bfloat16):
    drawn = spread * jax.random.normal(stream_key, extent, jnp.float32)
    if split:
        drawn = drawn * shard_levels(stream_key, extent, split, -0.22, 0.18)
    return jnp.clip(drawn, -most, most).astype(kind)


def setup_inputs(seed: int = 0) -> dict:
    keys = jax.random.split(jax.random.key(seed), 7)
    volume = bell_draw(keys[0], (SAMPLES, CIN, DEPTH, HEIGHT * WIDTH), 1.0, 6.0, ((0, 16), (2, 2)), jnp.float32)
    cotangent = bell_draw(keys[1], (SAMPLES, C2, (DEPTH // 4) * (HEIGHT // 4) * (WIDTH // 4)), 0.5, 6.0, ((0, 16), (1, 2)), jnp.float32)
    w_first = bell_draw(keys[2], (C1, CIN * 64), (CIN * 64) ** -0.5, 0.125, (), jnp.float32)
    b_first = bell_draw(keys[3], (C1,), 0.5, 3.0, (), jnp.float32)
    w_second = bell_draw(keys[4], (C2, C1 * 64), (C1 * 64) ** -0.5, 0.09375, ((0, 2),), jnp.float32)
    b_second = bell_draw(keys[5], (C2,), 0.5, 3.0, ((0, 2),), jnp.float32)
    return dict(volume=volume, cotangent=cotangent, w_first=w_first, b_first=b_first, w_second=w_second, b_second=b_second)


SLOPE = 0.3

def activate(pre_value):
    return SLOPE * pre_value + (1.0 - SLOPE) * jax.nn.softplus(pre_value)

def convolve(field, weight, bias_vector):
    out_count = weight.shape[0]
    kernel = weight.reshape(out_count, field.shape[1], 4, 4, 4)
    result = lax.conv_general_dilated(field, kernel, (2, 2, 2), [(1, 1), (1, 1), (1, 1)], dimension_numbers=('NCDHW', 'OIDHW', 'NCDHW'), precision=lax.Precision.HIGHEST)
    return result + bias_vector[None, :, None, None, None]

def reference(volume, cotangent, w_first, b_first, w_second, b_second):
    sample_count = volume.shape[0]
    volume_grid = volume.reshape(sample_count, CIN, DEPTH, HEIGHT, WIDTH)

    def forward(volume_grid, w_first, b_first, w_second, b_second):
        hidden = activate(convolve(volume_grid, w_first, b_first))
        return activate(convolve(hidden, w_second, b_second)).reshape(sample_count, C2, -1)
    output, pullback = jax.vjp(forward, volume_grid, w_first, b_first, w_second, b_second)
    grad_grid, grad_wone, grad_bone, grad_wtwo, grad_btwo = pullback(cotangent)
    sample_scale = 1.0 / SAMPLES
    return (output, grad_grid.reshape(volume.shape), grad_wone * sample_scale, grad_bone * sample_scale, grad_wtwo * sample_scale, grad_btwo * sample_scale)
```

```python
import functools

import jax
import jax.numpy as jnp
import numpy as np
from jax import lax
from jax.experimental import pallas as pl
from jax.experimental.pallas import tpu as pltpu
from jax.sharding import PartitionSpec as P

HEIGHT = 16
WIDTH = 16
SLOPE = 0.3
TAPS = 64
LANES = 128
VMEM_BYTES = 40 * 1024 * 1024
F32 = jnp.float32
BF16 = jnp.bfloat16


def activate(pre_value):
    tail = jnp.exp(-jnp.abs(pre_value))
    return SLOPE * pre_value + (1.0 - SLOPE) * (jnp.maximum(pre_value, 0.0) + jnp.log1p(tail))


def slope_of(pre_value):
    tail = jnp.exp(-jnp.abs(pre_value))
    return SLOPE + (1.0 - SLOPE) * (jnp.where(pre_value >= 0, 1.0, tail) / (1.0 + tail))


def halves(value):
    high = value.astype(BF16)
    return high, (value - high.astype(F32)).astype(BF16)


def dot(a, b):
    return lax.dot_general(a, b, (((1,), (0,)), ((), ())), preferred_element_type=F32)


def dot_nt(a, b):
    return lax.dot_general(a, b, (((1,), (1,)), ((), ())), preferred_element_type=F32)


def plane_picks(height, width):
    out_height, out_width = height // 2, width // 2
    picks = np.zeros((height, width, 4, 4, out_height, out_width), np.float32)
    for j in range(4):
        for l in range(4):
            for h in range(out_height):
                for k in range(out_width):
                    q, r = 2 * h + j - 1, 2 * k + l - 1
                    if 0 <= q < height and 0 <= r < width:
                        picks[q, r, j, l, h, k] = 1.0
    return picks.reshape(height * width, 16, out_height * out_width)


def pair_picks(height, width):
    one = plane_picks(height, width)
    cells, _, outs = one.shape
    both = np.zeros((2, cells, 16, 2, outs), np.float32)
    both[0, :, :, 0] = one
    both[1, :, :, 1] = one
    return both.reshape(2 * cells, 32 * outs)


def first_layer_kernel(slabs, place_ref, *refs):
    own_ref, far_ref, picks_ref, w_ref, b_ref, windows_ref, hidden_ref, slope_ref, planes_ref, columns_ref = refs
    channels, rows, _ = own_ref.shape
    planes = slabs * rows
    out_planes = planes // 2
    for p in range(planes):
        slab, row = p // rows, p % rows
        if slabs == 2:
            at_first = place_ref[0] == slab
            plane = jnp.where(at_first, own_ref[:, row, :], far_ref[:, row, :])
        else:
            plane = far_ref[slab, :, row, :]
        high, low = halves(plane)
        both = dot(jnp.concatenate([high, low], axis=0), picks_ref[...])
        planes_ref[p] = both[:channels] + both[channels:]
    outs = HEIGHT * WIDTH // 4
    empty = jnp.zeros((channels, outs), F32)
    for m in range(out_planes // 2):
        for i in range(4):
            for t in range(16):
                parts = []
                for p in (4 * m + i - 1, 4 * m + i + 1):
                    inside = 0 <= p < planes
                    parts.append(planes_ref[p, :, t * outs : (t + 1) * outs] if inside else empty)
                columns_ref[pl.ds(16 * i + t, channels, stride=TAPS), :] = jnp.concatenate(parts, axis=1)
        high, low = halves(columns_ref[...])
        windows_ref[m] = jnp.concatenate([high, low], axis=1)
        w_high, w_low = halves(w_ref[...])
        count = w_high.shape[0]
        product = dot(jnp.concatenate([w_high, w_low], axis=0), windows_ref[m])
        pre_value = (
            product[:count, :LANES] + product[:count, LANES:] + product[count:, :LANES] + b_ref[...]
        )
        hidden_ref[:, m * LANES : (m + 1) * LANES] = activate(pre_value)
        slope_ref[:, m * LANES : (m + 1) * LANES] = slope_of(pre_value)


def forward_second(windows, w, b, cotangent):
    count = w.shape[0]
    w_high, w_low = halves(w)
    stacked = jnp.concatenate([w_high, w_low], axis=0)
    pieces = []
    for value in windows:
        cells = value.shape[1] // 2
        product = dot(stacked, value)
        pieces.append(product[:count, :cells] + product[:count, cells:] + product[count:, :cells])
    pre_value = jnp.concatenate(pieces, axis=1) + b
    return pre_value, cotangent * slope_of(pre_value), w_high, w_low


def back_second(gradient, w_high, w_low):
    g_high, g_low = halves(gradient.T)
    return dot(
        jnp.concatenate([g_high, g_high, g_low], axis=1),
        jnp.concatenate([w_high, w_low, w_high], axis=0),
    )


def second_layer_kernel(scale, hidden_ref, picks_ref, w_ref, b_ref, cot_ref, *refs):
    output_ref, payload_ref, windows_ref, back_ref, columns_ref = refs
    channels, length = hidden_ref.shape
    picks = picks_ref[...]
    plane = picks.shape[0] // 2
    cells = picks.shape[1] // 16
    planes = length // plane
    pairs = planes // 4
    empty = jnp.zeros((channels, plane), F32)
    hidden = hidden_ref[...]
    for m in range(pairs):
        for i in range(4):
            parts = []
            for p in (4 * m + i - 1, 4 * m + i + 1):
                parts.append(hidden[:, p * plane : (p + 1) * plane] if 0 <= p < planes else empty)
            high, low = halves(jnp.concatenate(parts, axis=1))
            both = dot(jnp.concatenate([high, low], axis=0), picks)
            picked = both[:channels] + both[channels:]
            per_tile = LANES // cells
            for t in range(16):
                tile = picked[:, t // per_tile * LANES : (t // per_tile + 1) * LANES]
                turn = t % per_tile * cells
                if turn:
                    tile = pltpu.roll(tile, LANES - turn, 1)
                columns_ref[pl.ds(16 * i + t, channels, stride=TAPS), :] = tile
        high, low = halves(columns_ref[:, :cells])
        windows_ref[m] = jnp.concatenate([high, low], axis=1)
    windows = [windows_ref[m] for m in range(pairs)]
    pre_value, gradient, w_high, w_low = forward_second(windows, w_ref[...], b_ref[...], cot_ref[...])
    output_ref[...] = activate(pre_value)
    back_ref[...] = back_second(gradient, w_high, w_low)
    count = gradient.shape[0]
    half = channels * TAPS // 2
    total = None
    for m in range(pairs):
        g_high, g_low = halves(gradient[:, m * cells : (m + 1) * cells])
        top = jnp.concatenate([g_high, g_high], axis=1)
        bottom = jnp.concatenate([g_low, jnp.zeros_like(g_low)], axis=1)
        product = dot_nt(jnp.concatenate([top, bottom], axis=0), windows[m])
        product = product[:count] + product[count:]
        total = product if total is None else total + product
    total = total * scale
    payload_ref[:count, :half] = total[:, :half]
    payload_ref[count:, :half] = total[:, half:]
    sums = jnp.sum(gradient, axis=1, keepdims=True) * scale
    payload_ref[:count, half:] = jnp.broadcast_to(sums, (count, LANES))
    payload_ref[count:, half:] = jnp.zeros((count, LANES), F32)


def middle_kernel(scale, slabs, place_ref, *refs):
    (near_ref, far_ref, back_ref, windows_two_ref, windows_one_ref, slope_ref, picks_ref,
     grad_ref, payload_ref, columns_ref, rows_ref) = refs
    channels, length = slope_ref.shape
    taps_all = channels * TAPS
    pairs = windows_two_ref.shape[0]
    total_cells = pairs * windows_two_ref.shape[2] // 2
    cells = total_cells // pairs
    if slabs == 2:
        first = place_ref[1] == 0
        near, far = near_ref[...], far_ref[...]
        table = jnp.concatenate([jnp.where(first, near, far), jnp.where(first, far, near)], axis=0)
        extra = near[:, taps_all:]
        parts = [extra[:, :total_cells], extra[:, total_cells : 2 * total_cells]]
        cotangent = jnp.concatenate(parts, axis=0)
        b = table[:, taps_all + 2 * total_cells : taps_all + 2 * total_cells + 1]
    else:
        table = far_ref[...]
        cotangent = table[:, taps_all : taps_all + total_cells]
        b = table[:, taps_all + total_cells : taps_all + total_cells + 1]
    w = table[:, :taps_all]
    windows = [windows_two_ref[m] for m in range(pairs)]
    _, gradient, w_high, w_low = forward_second(windows, w, b, cotangent)
    back = back_second(gradient, w_high, w_low)
    if slabs == 2:
        back = back + back_ref[...]
    plane = picks_ref.shape[1] // 2
    planes = length // plane
    per_tile = LANES // cells
    lane = lax.broadcasted_iota(jnp.int32, (channels, LANES), 1)
    sums = [None] * planes
    for m in range(pairs):
        columns_ref[:, :cells] = back[m * cells : (m + 1) * cells, :].T
        for i in range(4):
            for g in range(16 // per_tile):
                tile = None
                for s in range(per_tile):
                    part = columns_ref[pl.ds(16 * i + g * per_tile + s, channels, stride=TAPS), :]
                    if s:
                        part = pltpu.roll(part, s * cells, 1)
                    tile = part if tile is None else jnp.where(lane >= s * cells, part, tile)
                rows_ref[:, g * LANES : (g + 1) * LANES] = tile
            high, low = halves(rows_ref[...])
            both = dot(jnp.concatenate([high, low], axis=0), picks_ref[...])
            both = both[:channels] + both[channels:]
            for at, p in enumerate((4 * m + i - 1, 4 * m + i + 1)):
                if 0 <= p < planes:
                    piece = both[:, at * plane : (at + 1) * plane]
                    sums[p] = piece if sums[p] is None else sums[p] + piece
    gradient = jnp.concatenate(sums, axis=1) * slope_ref[...]
    grad_ref[...] = gradient
    total = None
    for m in range(length // LANES):
        g_high, g_low = halves(gradient[:, m * LANES : (m + 1) * LANES])
        top = jnp.concatenate([g_high, g_high], axis=1)
        bottom = jnp.concatenate([g_low, jnp.zeros_like(g_low)], axis=1)
        product = dot_nt(jnp.concatenate([top, bottom], axis=0), windows_one_ref[m])
        product = product[:channels] + product[channels:]
        total = product if total is None else total + product
    width = total.shape[1]
    payload_ref[:, :width] = total * scale
    totals = jnp.sum(gradient, axis=1, keepdims=True) * scale
    payload_ref[:, width:] = jnp.broadcast_to(totals, (channels, LANES))


def volume_kernel(grad_ref, w_ref, picks_ref, out_ref, columns_ref, rows_ref):
    channels, rows, _ = out_ref.shape
    count, length = grad_ref.shape
    g_high, g_low = halves(grad_ref[...])
    w_high, w_low = halves(w_ref[...])
    right = jnp.concatenate(
        [
            jnp.concatenate([g_high, g_low], axis=1),
            jnp.concatenate([g_high, jnp.zeros_like(g_low)], axis=1),
        ],
        axis=0,
    )
    product = dot(jnp.concatenate([w_high, w_low], axis=1), right)
    product = product[:, :length] + product[:, length:]
    for m in range(length // LANES):
        columns_ref[m] = product[:, m * LANES : (m + 1) * LANES]
    outs = HEIGHT * WIDTH // 4
    for p in range(rows):
        for t in range(16):
            piece = None
            for i in ((p + 1) % 2, (p + 1) % 2 + 2):
                d = (p + 1 - i) // 2 + 1
                tile = columns_ref[d // 2, pl.ds(16 * i + t, channels, stride=TAPS), :]
                at = d % 2 * outs
                part = tile[:, at : at + outs]
                piece = part if piece is None else piece + part
            rows_ref[p * channels : (p + 1) * channels, t * outs : (t + 1) * outs] = piece
    high, low = halves(rows_ref[...])
    both = dot(jnp.concatenate([high, low], axis=0), picks_ref[...])
    both = both[: rows * channels] + both[rows * channels :]
    for p in range(rows):
        out_ref[:, p, :] = both[p * channels : (p + 1) * channels]


def call(kernel, outs, scratch, *args, scalars=0):
    vmem = pl.BlockSpec(memory_space=pltpu.VMEM)
    smem = pl.BlockSpec(memory_space=pltpu.SMEM)
    shapes = [jax.ShapeDtypeStruct(s, d) for s, d in outs]
    return pl.pallas_call(
        kernel,
        out_shape=shapes,
        in_specs=[smem] * scalars + [vmem] * (len(args) - scalars),
        out_specs=[vmem] * len(shapes),
        scratch_shapes=[pltpu.VMEM(s, d) for s, d in scratch],
        compiler_params=pltpu.CompilerParams(vmem_limit_bytes=VMEM_BYTES),
        cost_estimate=pl.CostEstimate(flops=1 << 20, bytes_accessed=1 << 18, transcendentals=0),
    )(*args)


def swap(value, axis, bit):
    count = lax.axis_size(axis)
    return lax.ppermute(value, axis, [(i, i ^ bit) for i in range(count)])


def summed(value, bits, depth):
    count = lax.axis_size("dp")
    if count & (count - 1):
        return lax.psum(value, "dp")
    place = lax.axis_index("dp")
    for bit in bits[:depth]:
        upper = (place >> bit) & 1
        half = value.shape[0] // 2
        sent = lax.dynamic_slice_in_dim(value, (1 - upper) * half, half, axis=0)
        kept = lax.dynamic_slice_in_dim(value, upper * half, half, axis=0)
        value = kept + swap(sent, "dp", 1 << bit)
    for bit in bits[depth:]:
        value = value + swap(value, "dp", 1 << bit)
    for bit in reversed(bits[:depth]):
        upper = (place >> bit) & 1
        other = swap(value, "dp", 1 << bit)
        value = jnp.concatenate(
            [jnp.where(upper == 0, value, other), jnp.where(upper == 0, other, value)], axis=0
        )
    return value


def on_device(volume, cotangent, w_first, b_first, w_second, b_second):
    _, in_channels, slab_rows, plane_cells = volume.shape
    mid_channels = w_first.shape[0]
    own_count = w_second.shape[0]
    slabs = lax.axis_size("space")
    dp_size = lax.axis_size("dp")
    scale = 1.0 / dp_size
    place = lax.axis_index("space")
    core = lax.axis_index("dp") & 1
    places = jnp.stack([place, core]).astype(jnp.int32)
    planes = slabs * slab_rows
    mid_planes = planes // 2
    mid_cells = plane_cells // 4
    out_cells = mid_planes // 2 * (mid_cells // 4)
    taps_one, taps_two = in_channels * TAPS, mid_channels * TAPS

    picks_one = plane_picks(HEIGHT, WIDTH).reshape(plane_cells, 16 * mid_cells)
    picks_two = pair_picks(HEIGHT // 2, WIDTH // 2)
    pick_one, pick_one_t = jnp.asarray(picks_one, BF16), jnp.asarray(picks_one.T.copy(), BF16)
    pick_two, pick_two_t = jnp.asarray(picks_two, BF16), jnp.asarray(picks_two.T.copy(), BF16)

    own_volume = volume[0]
    own_cot = cotangent[0]
    if slabs == 2:
        far_volume = swap(own_volume, "space", 1)
        part = own_count // 2
        rows = jnp.concatenate([w_second, b_second[:, None]], axis=1)
        rows = lax.dynamic_slice_in_dim(rows, core * part, part, axis=0)
        spare = -(2 * out_cells + 1) % LANES
        sent = jnp.concatenate(
            [
                rows[:, :taps_two],
                own_cot[:part],
                own_cot[part:],
                rows[:, taps_two:],
                jnp.zeros((part, spare), F32),
            ],
            axis=1,
        )
        near_table = swap(sent, "space", 1)
        far_table = swap(near_table, "dp", 1)
    else:
        far_volume = lax.all_gather(own_volume, "space", axis=0)
        table = jnp.concatenate([w_second, own_cot, b_second[:, None]], axis=1)
        table = jnp.pad(table, ((0, 0), (0, -table.shape[1] % LANES)))
        far_table = lax.all_gather(table, "space", axis=0, tiled=True)
        near_table = table

    pairs = mid_planes // 2
    windows_one, hidden, slope_one = call(
        functools.partial(first_layer_kernel, slabs),
        [
            ((pairs, taps_one, 2 * LANES), BF16),
            ((mid_channels, mid_planes * mid_cells), F32),
            ((mid_channels, mid_planes * mid_cells), F32),
        ],
        [((planes, in_channels, 16 * mid_cells), F32), ((taps_one, LANES), F32)],
        places, own_volume, far_volume, pick_one, w_first, b_first[:, None],
        scalars=1,
    )

    pairs_two = mid_planes // 4
    cells = out_cells // pairs_two
    output, payload_two, windows_two, back = call(
        functools.partial(second_layer_kernel, scale),
        [
            ((own_count, out_cells), F32),
            ((2 * own_count, taps_two // 2 + LANES), F32),
            ((pairs_two, taps_two, 2 * cells), BF16),
            ((out_cells, taps_two), F32),
        ],
        [((taps_two, LANES), F32)],
        hidden, pick_two, w_second, b_second[:, None], own_cot,
    )
    bits = range(dp_size.bit_length() - 1)
    order_two = list(bits)
    order_one = [0] + list(bits)[1:3][::-1] + list(bits)[3:]
    sum_two = summed(payload_two, order_two, 3)

    grad_first, payload_one = call(
        functools.partial(middle_kernel, scale, slabs),
        [
            ((mid_channels, mid_planes * mid_cells), F32),
            ((mid_channels, taps_one + LANES), F32),
        ],
        [((taps_two, LANES), F32), ((mid_channels, 16 * cells), F32)],
        places, near_table, far_table, back, windows_two, windows_one, slope_one, pick_two_t,
        scalars=1,
    )
    sum_one = summed(payload_one, order_one, 3)

    window_cells = (slab_rows // 2 + 2) * mid_cells
    framed = jnp.pad(grad_first, ((0, 0), (mid_cells, mid_cells)))
    around = lax.dynamic_slice_in_dim(
        framed, place * (slab_rows // 2 * mid_cells), window_cells, axis=1
    )
    (grad_volume,) = call(
        volume_kernel,
        [((in_channels, slab_rows, plane_cells), F32)],
        [
            ((window_cells // LANES, taps_one, LANES), F32),
            ((slab_rows * in_channels, 16 * mid_cells), F32),
        ],
        around, w_first.T, pick_one_t,
    )

    half = taps_two // 2
    grad_w_second = jnp.concatenate([sum_two[:own_count, :half], sum_two[own_count:, :half]], axis=1)
    grad_b_second = sum_two[:own_count, half]
    grad_w_first = sum_one[:, :taps_one]
    grad_b_first = sum_one[:, taps_one]
    return (output[None], grad_volume[None], grad_w_first, grad_b_first, grad_w_second, grad_b_second)


def solution(mesh):
    in_specs = (
        P("dp", None, "space", None),
        P("dp", "space", None),
        P(),
        P(),
        P("space", None),
        P("space"),
    )
    out_specs = (
        P("dp", "space", None),
        P("dp", None, "space", None),
        P(),
        P(),
        P("space", None),
        P("space"),
    )
    return jax.shard_map(
        on_device, mesh=mesh, in_specs=in_specs, out_specs=out_specs, check_vma=False
    )
```

```python
import functools
import math

import jax
import jax.numpy as jnp
from jax import lax
from jax.experimental import pallas as pl
from jax.experimental.pallas import tpu as pltpu
from jax.sharding import PartitionSpec as P

HEIGHT = 16
WIDTH = 16
SLOPE = 0.3
TAPS = 64
LANES = 128
F32 = jnp.float32
BF16 = jnp.bfloat16


def activate(pre_value):
    tail = jnp.exp(-jnp.abs(pre_value))
    return SLOPE * pre_value + (1.0 - SLOPE) * (jnp.maximum(pre_value, 0.0) + jnp.log1p(tail))


def slope_of(pre_value):
    tail = jnp.exp(-jnp.abs(pre_value))
    return SLOPE + (1.0 - SLOPE) * (jnp.where(pre_value >= 0, 1.0, tail) / (1.0 + tail))


def halves(value):
    high = value.astype(BF16)
    return high, (value - high.astype(F32)).astype(BF16)


def dot(a, b):
    return lax.dot_general(a, b, (((1,), (0,)), ((), ())), preferred_element_type=F32)


def dot_nt(a, b):
    return lax.dot_general(a, b, (((1,), (1,)), ((), ())), preferred_element_type=F32)


def bits_of(size):
    return size.bit_length() - 1


def picks(height, width, planes):
    lane_bits, row_bits = bits_of(width // 2), bits_of(height // 2)
    cell_bits, tap_bits = lane_bits + row_bits, lane_bits + row_bits + bits_of(planes)
    columns = 16 << tap_bits
    at = lax.broadcasted_iota(jnp.int32, (1, columns), 1)
    k, h = at & (width // 2 - 1), (at >> lane_bits) & (height // 2 - 1)
    q = 2 * h + ((at >> (tap_bits + 2)) & 3) - 1
    r = 2 * k + ((at >> tap_bits) & 3) - 1
    inside = (q >= 0) & (q < height) & (r >= 0) & (r < width)
    plane = (at >> cell_bits) & (planes - 1)
    target = jnp.where(inside, plane * height * width + q * width + r, -1)
    row = lax.broadcasted_iota(jnp.int32, (planes * height * width, columns), 0)
    return jnp.where(row == target, 1.0, 0.0).astype(BF16)


def as_column(row):
    count = row.shape[1]
    across = lax.broadcasted_iota(jnp.int32, (count, count), 1)
    down = lax.broadcasted_iota(jnp.int32, (count, count), 0)
    return jnp.sum(jnp.where(across == down, row, 0.0), axis=1, keepdims=True)


def picked_planes(planes):
    high, low = halves(jnp.concatenate(planes, axis=0))
    both = dot(jnp.concatenate([high, low], axis=0), picks(HEIGHT, WIDTH, 1))
    count = high.shape[0]
    return both[:count] + both[count:]


def slab_kernel(slab_ref, planes_ref):
    channels, rows, _ = slab_ref.shape
    planes = picked_planes([slab_ref[:, row, :] for row in range(rows)])
    for row in range(rows):
        planes_ref[row] = planes[row * channels : (row + 1) * channels]


def first_layer_kernel(slabs, place_ref, own_ref, far_ref, w_hbm, b_ref, *refs):
    windows_ref, hidden_ref, slope_ref, planes_ref, columns_ref, w_ref, own_sem, w_sem = refs
    w_copy = pltpu.make_async_copy(w_hbm, w_ref, w_sem)
    w_copy.start()
    _, channels, rows, _ = far_ref.shape
    planes = slabs * rows
    if slabs == 2:
        place = place_ref[0]
        own_copy = pltpu.make_async_copy(own_ref, planes_ref.at[pl.ds(place * rows, rows)], own_sem)
        own_copy.start()
        far = picked_planes([far_ref[0, :, row, :] for row in range(rows)])
        for row in range(rows):
            planes_ref[(1 - place) * rows + row] = far[row * channels : (row + 1) * channels]
        own_copy.wait()
    else:
        for slab in range(slabs):
            far = picked_planes([far_ref[slab, :, row, :] for row in range(rows)])
            for row in range(rows):
                planes_ref[slab * rows + row] = far[row * channels : (row + 1) * channels]
    outs = HEIGHT * WIDTH // 4
    empty = jnp.zeros((channels, outs), F32)
    b = as_column(b_ref[...])
    w_copy.wait()
    w_high, w_low = halves(w_ref[...])
    count = w_high.shape[0]
    stacked = jnp.concatenate([w_high, w_low], axis=0)
    for m in range(planes // 4):
        for i in range(4):
            for t in range(16):
                parts = []
                for p in (4 * m + i - 1, 4 * m + i + 1):
                    inside = 0 <= p < planes
                    parts.append(planes_ref[p, :, t * outs : (t + 1) * outs] if inside else empty)
                columns_ref[pl.ds(16 * i + t, channels, stride=TAPS), :] = jnp.concatenate(parts, axis=1)
        high, low = halves(columns_ref[...])
        windows_ref[m] = jnp.concatenate([high, low], axis=1)
        product = dot(stacked, windows_ref[m])
        pre_value = product[:count, :LANES] + product[:count, LANES:] + product[count:, :LANES] + b
        hidden_ref[:, m * LANES : (m + 1) * LANES] = activate(pre_value)
        slope_ref[:, m * LANES : (m + 1) * LANES] = slope_of(pre_value)


def forward_second(windows, w, b, cotangent):
    count = w.shape[0]
    w_high, w_low = halves(w)
    stacked = jnp.concatenate([w_high, w_low], axis=0)
    pieces = []
    for value in windows:
        cells = value.shape[1] // 2
        product = dot(stacked, value)
        pieces.append(product[:count, :cells] + product[:count, cells:] + product[count:, :cells])
    pre_value = jnp.concatenate(pieces, axis=1) + b
    return pre_value, cotangent * slope_of(pre_value), w_high, w_low


def back_second(gradient, w_high, w_low):
    g_high, g_low = halves(gradient.T)
    return dot(
        jnp.concatenate([g_high, g_high, g_low], axis=1),
        jnp.concatenate([w_high, w_low, w_high], axis=0),
    )


def second_layer_kernel(hidden_ref, w_hbm, b_ref, cot_ref, *refs):
    output_ref, grad_ref, back_ref, windows_ref, columns_ref, rows_ref, w_ref, w_sem = refs
    w_copy = pltpu.make_async_copy(w_hbm, w_ref, w_sem)
    w_copy.start()
    channels, length = hidden_ref.shape
    pair = picks(HEIGHT // 2, WIDTH // 2, 2)
    plane = pair.shape[0] // 2
    cells = pair.shape[1] // 16
    planes = length // plane
    pairs = planes // 4
    per_tile = LANES // cells
    empty = jnp.zeros((channels, plane), F32)
    hidden = hidden_ref[...]
    sides = []
    for m in range(pairs):
        for i in range(4):
            parts = []
            for p in (4 * m + i - 1, 4 * m + i + 1):
                parts.append(hidden[:, p * plane : (p + 1) * plane] if 0 <= p < planes else empty)
            sides.append(jnp.concatenate(parts, axis=1))
    high, low = halves(jnp.concatenate(sides, axis=0))
    both = dot(jnp.concatenate([high, low], axis=0), pair)
    picked = both[: high.shape[0]] + both[high.shape[0] :]
    for m in range(pairs):
        for i in range(4):
            at = (4 * m + i) * channels
            for t in range(16):
                tile = picked[at : at + channels, t // per_tile * LANES : (t // per_tile + 1) * LANES]
                turn = t % per_tile * cells
                if turn:
                    tile = pltpu.roll(tile, LANES - turn, 1)
                columns_ref[pl.ds(16 * i + t, channels, stride=TAPS), :] = tile
        high, low = halves(columns_ref[:, :cells])
        windows_ref[m] = jnp.concatenate([high, low], axis=1)
    windows = [windows_ref[m] for m in range(pairs)]
    w_copy.wait()
    pre_value, gradient, w_high, w_low = forward_second(
        windows, w_ref[...], as_column(b_ref[...]), cot_ref[...]
    )
    output_ref[...] = activate(pre_value)
    grad_ref[...] = gradient
    back = back_second(gradient, w_high, w_low)
    lane = lax.broadcasted_iota(jnp.int32, (channels, LANES), 1)
    for m in range(pairs):
        columns_ref[:, :cells] = back[m * cells : (m + 1) * cells, :].T
        for i in range(4):
            at = (4 * m + i) * channels
            for g in range(16 // per_tile):
                tile = None
                for s in range(per_tile):
                    part = columns_ref[pl.ds(16 * i + g * per_tile + s, channels, stride=TAPS), :]
                    if s:
                        part = pltpu.roll(part, s * cells, 1)
                    tile = part if tile is None else jnp.where(lane >= s * cells, part, tile)
                rows_ref[at : at + channels, g * LANES : (g + 1) * LANES] = tile
    high, low = halves(rows_ref[...])
    both = dot_nt(jnp.concatenate([high, low], axis=0), pair)
    both = both[: high.shape[0]] + both[high.shape[0] :]
    sums = [None] * planes
    for m in range(pairs):
        for i in range(4):
            at = (4 * m + i) * channels
            for side, p in enumerate((4 * m + i - 1, 4 * m + i + 1)):
                if 0 <= p < planes:
                    piece = both[at : at + channels, side * plane : (side + 1) * plane]
                    sums[p] = piece if sums[p] is None else sums[p] + piece
    back_ref[...] = jnp.concatenate(sums, axis=1)


def kernel_gradient(scale, gradient, windows):
    count = gradient.shape[0]
    cells = windows[0].shape[1] // 2
    total = None
    for m, window in enumerate(windows):
        g_high, g_low = halves(gradient[:, m * cells : (m + 1) * cells])
        top = jnp.concatenate([g_high, g_high], axis=1)
        bottom = jnp.concatenate([g_low, jnp.zeros_like(g_low)], axis=1)
        product = dot_nt(jnp.concatenate([top, bottom], axis=0), window)
        product = product[:count] + product[count:]
        total = product if total is None else total + product
    return total * scale, jnp.sum(gradient, axis=1, keepdims=True) * scale


def second_kernel_gradient(scale, grad_ref, windows_ref, payload_ref):
    windows = [windows_ref[m] for m in range(windows_ref.shape[0])]
    total, sums = kernel_gradient(scale, grad_ref[...], windows)
    count, width = total.shape
    half = width // 2
    payload_ref[:count, :half] = total[:, :half]
    payload_ref[count:, :half] = total[:, half:]
    payload_ref[:count, half:] = jnp.broadcast_to(sums, (count, LANES))
    payload_ref[count:, half:] = jnp.zeros((count, LANES), F32)


def first_kernel_gradient(scale, shares, *refs):
    slope_ref, windows_ref, grad_ref, payload_ref = refs[shares:]
    gradient = refs[0][...]
    for share in refs[1:shares]:
        gradient = gradient + share[...]
    gradient = gradient * slope_ref[...]
    grad_ref[...] = gradient
    windows = [windows_ref[m] for m in range(windows_ref.shape[0])]
    total, sums = kernel_gradient(scale, gradient, windows)
    count, width = total.shape
    payload_ref[:, :width] = total
    payload_ref[:, width:] = jnp.broadcast_to(sums, (count, LANES))


def volume_kernel(grad_ref, w_ref, out_ref, columns_ref, rows_ref):
    channels, rows, _ = out_ref.shape
    count, length = grad_ref.shape
    g_high, g_low = halves(grad_ref[...])
    w_high, w_low = halves(w_ref[...])
    right = jnp.concatenate(
        [
            jnp.concatenate([g_high, g_low], axis=1),
            jnp.concatenate([g_high, jnp.zeros_like(g_low)], axis=1),
        ],
        axis=0,
    )
    product = dot(jnp.concatenate([w_high, w_low], axis=1), right)
    product = product[:, :length] + product[:, length:]
    for m in range(length // LANES):
        columns_ref[m] = product[:, m * LANES : (m + 1) * LANES]
    outs = HEIGHT * WIDTH // 4
    for p in range(rows):
        for t in range(16):
            piece = None
            for i in ((p + 1) % 2, (p + 1) % 2 + 2):
                d = (p + 1 - i) // 2 + 1
                tile = columns_ref[d // 2, pl.ds(16 * i + t, channels, stride=TAPS), :]
                at = d % 2 * outs
                part = tile[:, at : at + outs]
                piece = part if piece is None else piece + part
            rows_ref[p * channels : (p + 1) * channels, t * outs : (t + 1) * outs] = piece
    high, low = halves(rows_ref[...])
    both = dot_nt(jnp.concatenate([high, low], axis=0), picks(HEIGHT, WIDTH, 1))
    both = both[: rows * channels] + both[rows * channels :]
    for p in range(rows):
        out_ref[:, p, :] = both[p * channels : (p + 1) * channels]


def call(kernel, outs, scratch, *args, spaces=""):
    kinds = {"v": pltpu.VMEM, "s": pltpu.SMEM, "h": pl.ANY}
    specs = [pl.BlockSpec(memory_space=kinds[k]) for k in spaces.ljust(len(args), "v")]
    shapes = [jax.ShapeDtypeStruct(s, d) for s, d in outs]
    held = sum(4 * math.prod(s) for s in [a.shape for a in args] + [s for s, _ in outs])
    held += sum(4 * math.prod(s) for s, d in scratch if d is not None)
    limit = max(2 * held, 8 << 20) if held < 8 << 20 else 56 << 20
    return pl.pallas_call(
        kernel,
        out_shape=shapes,
        in_specs=specs,
        out_specs=[pl.BlockSpec(memory_space=pltpu.VMEM)] * len(shapes),
        scratch_shapes=[s if d is None else pltpu.VMEM(s, d) for s, d in scratch],
        compiler_params=pltpu.CompilerParams(vmem_limit_bytes=limit),
        cost_estimate=pl.CostEstimate(flops=1 << 20, bytes_accessed=1 << 18, transcendentals=0),
    )(*args)


def swap(value, axis, bit):
    count = lax.axis_size(axis)
    return lax.ppermute(value, axis, [(i, i ^ bit) for i in range(count)])


def steps_of(value, bits, depth):
    place = lax.axis_index("dp")
    for bit in bits[:depth]:
        upper = (place >> bit) & 1
        half = value.shape[0] // 2
        value = yield value
        sent = lax.dynamic_slice_in_dim(value, (1 - upper) * half, half, axis=0)
        kept = lax.dynamic_slice_in_dim(value, upper * half, half, axis=0)
        value = kept + swap(sent, "dp", 1 << bit)
    for bit in bits[depth:]:
        value = yield value
        value = value + swap(value, "dp", 1 << bit)
    for bit in reversed(bits[:depth]):
        upper = (place >> bit) & 1
        value = yield value
        other = swap(value, "dp", 1 << bit)
        value = jnp.concatenate(
            [jnp.where(upper == 0, value, other), jnp.where(upper == 0, other, value)], axis=0
        )
    return value


def sums_over_dp(first, second, order_first, order_second, depth):
    count = lax.axis_size("dp")
    if count & (count - 1):
        return lax.psum(first, "dp"), lax.psum(second, "dp")
    runs = [steps_of(second, order_second, depth), steps_of(first, order_first, depth)]
    values = [next(run) for run in runs]
    behind = None
    while True:
        try:
            operand = values[0]
            if behind is not None:
                operand, behind = lax.optimization_barrier((operand, behind))
            values[0] = runs[0].send(operand)
            behind = values[1]
            ahead = values[0]
        except StopIteration as stop:
            done_second = stop.value
            ahead = done_second
        try:
            values[1] = runs[1].send(values[1])
        except StopIteration as stop:
            return stop.value, done_second


def on_device(volume, cotangent, w_first, b_first, w_second, b_second):
    _, in_channels, slab_rows, plane_cells = volume.shape
    mid_channels = w_first.shape[0]
    own_count = w_second.shape[0]
    slabs = lax.axis_size("space")
    dp_size = lax.axis_size("dp")
    scale = 1.0 / dp_size
    place = lax.axis_index("space")
    planes = slabs * slab_rows
    mid_planes = planes // 2
    mid_cells = plane_cells // 4
    mid_length = mid_planes * mid_cells
    out_cells = mid_planes // 2 * (mid_cells // 4)
    taps_one, taps_two = in_channels * TAPS, mid_channels * TAPS
    semaphore = (pltpu.SemaphoreType.DMA, None)

    own_volume = volume[0]
    if slabs == 2:
        far_volume = swap(own_volume, "space", 1)[None]
        (own_planes,) = call(
            slab_kernel, [((slab_rows, in_channels, 16 * mid_cells), F32)], [], own_volume
        )
    else:
        far_volume = lax.all_gather(own_volume, "space", axis=0)
        own_planes = own_volume
    pairs = mid_planes // 2
    windows_one, hidden, slope_one = call(
        functools.partial(first_layer_kernel, slabs),
        [
            ((pairs, taps_one, 2 * LANES), BF16),
            ((mid_channels, mid_length), F32),
            ((mid_channels, mid_length), F32),
        ],
        [
            ((planes, in_channels, 16 * mid_cells), F32),
            ((taps_one, LANES), F32),
            (w_first.shape, F32),
            semaphore,
            semaphore,
        ],
        place.astype(jnp.int32)[None], own_planes, far_volume, w_first, b_first[None, :],
        spaces="svvh",
    )

    pairs_two = mid_planes // 4
    cells = out_cells // pairs_two
    output, grad_second, share, windows_two = call(
        second_layer_kernel,
        [
            ((own_count, out_cells), F32),
            ((own_count, out_cells), F32),
            ((mid_channels, mid_length), F32),
            ((pairs_two, taps_two, 2 * cells), BF16),
        ],
        [
            ((taps_two, LANES), F32),
            ((4 * pairs_two * mid_channels, 16 * cells), F32),
            (w_second.shape, F32),
            semaphore,
        ],
        hidden, w_second, b_second[None, :], cotangent[0],
        spaces="vh",
    )
    if slabs == 2:
        shares = [share, swap(share, "space", 1)]
    else:
        shares = [lax.psum(share, "space")]
    (payload_two,) = call(
        functools.partial(second_kernel_gradient, scale),
        [((2 * own_count, taps_two // 2 + LANES), F32)],
        [],
        grad_second, windows_two,
    )
    grad_first, payload_one = call(
        functools.partial(first_kernel_gradient, scale, len(shares)),
        [((mid_channels, mid_length), F32), ((mid_channels, taps_one + LANES), F32)],
        [],
        *shares, slope_one, windows_one,
    )
    bits = list(range(dp_size.bit_length() - 1))
    order_one = bits[:1] + bits[1:3][::-1] + bits[3:]
    sum_one, sum_two = sums_over_dp(payload_one, payload_two, order_one, bits, 3)

    window_cells = (slab_rows // 2 + 2) * mid_cells
    framed = jnp.pad(grad_first, ((0, 0), (mid_cells, mid_cells)))
    around = lax.dynamic_slice_in_dim(
        framed, place * (slab_rows // 2 * mid_cells), window_cells, axis=1
    )
    (grad_volume,) = call(
        volume_kernel,
        [((in_channels, slab_rows, plane_cells), F32)],
        [
            ((window_cells // LANES, taps_one, LANES), F32),
            ((slab_rows * in_channels, 16 * mid_cells), F32),
        ],
        around, w_first.T,
    )

    half = taps_two // 2
    grad_w_second = jnp.concatenate([sum_two[:own_count, :half], sum_two[own_count:, :half]], axis=1)
    grad_b_second = sum_two[:own_count, half]
    grad_w_first = sum_one[:, :taps_one]
    grad_b_first = sum_one[:, taps_one]
    return (output[None], grad_volume[None], grad_w_first, grad_b_first, grad_w_second, grad_b_second)


def solution(mesh):
    in_specs = (
        P("dp", None, "space", None),
        P("dp", "space", None),
        P(),
        P(),
        P("space", None),
        P("space"),
    )
    out_specs = (
        P("dp", "space", None),
        P("dp", None, "space", None),
        P(),
        P(),
        P("space", None),
        P("space"),
    )
    return jax.shard_map(
        on_device, mesh=mesh, in_specs=in_specs, out_specs=out_specs, check_vma=False
    )
```
